1024 devices in a mesh: sub: 32 (over y, z_hi), con: 32 (over x, z_lo, core).
Axes of the slice: x: 4, y: 8, z: 16 (z_hi: 4, z_lo: 4; z = z_hi * 4 + z_lo), core: 2. Of those that a mesh axis runs over, the one named last changes fastest.
Arguments:
- free_velocity: float32 [6, 65536], P(None, 'sub'), may hold values from -6 to 6
- inverse_mass: float32 [6, 65536], P(None, 'sub'), may hold values from 0.25 to 1
- contact_pair: int32 [2, 524288], P(None, ('sub', 'con')), may hold values from 0 to 2047, as said below
- jac_near: float32 [3, 6, 524288], P(None, None, ('sub', 'con')), may hold values from -2.5 to 2.5
- jac_far: float32 [3, 6, 524288], P(None, None, ('sub', 'con')), may hold values from -2.5 to 2.5
- inverse_delassus: float32 [3, 3, 524288], P(None, None, ('sub', 'con')), may hold values from -0.05 to 0.3
- friction: float32 [524288], P(('sub', 'con')), may hold values from 0.3 to 0.9
- velocity_bias: float32 [3, 524288], P(None, ('sub', 'con')), may hold values from -6 to 6
- warm_reaction: float32 [3, 524288], P(None, ('sub', 'con')), may hold values from -2 to 2
- active_flag: int32 [524288], P(('sub', 'con')), may hold values 0 or 1
- sticking_flag: int32 [524288], P(('sub', 'con')), may hold values 0 or 1
- next_list: int32 [32, 256], P('sub'), may hold values from 0 to 2048, as said below
- prev_list: int32 [32, 256], P('sub'), may hold values from 0 to 2048, as said below
Outputs:
- velocity: float32 [6, 65536], P(None, 'sub')
- reaction: float32 [3, 524288], P(None, ('sub', 'con'))
The draws below stay inside these ranges and needn't reach their ends.
Inputs may be any that keep to these rules, and one draw needn't show every extreme that they name: `contact_pair`: the two bodies of a contact differ. non-empty slots of a row come first and name distinct bodies; slot k of next_list row s is empty exactly when slot k of prev_list row s + 1 is; the last row of next_list and the first row of prev_list are empty; at least half of each other row's slots are filled, and some row has all 256 filled. `prev_list`: see next_list.
All inputs are finite; a program needn't handle non-finite values. No bound on the sum of `active_flag` or of `sticking_flag` on one device may be relied on, other than what follows from the above.
Results may differ from the reference program's by a relative error of at most 0.0001.
Values sent between devices are 32-bit elements; how exact they have to be, the bound alone decides.
A program may use at most 32 MiB of HBM per device.

```python
import math
import jax
import jax.numpy as jnp

B_SUB = 2048
C_DEV = 512
IF_CAP = 256
PASSES = 3
SUBDOMAINS = 32
BODIES = 65536
CONTACTS = 524288
N_CON = 32


def interface_lists(key):
    key_count, key_spot, key_next, key_prev = jax.random.split(key, 4)
    pairs = SUBDOMAINS - 1
    counts = jax.random.randint(key_count, (pairs,), IF_CAP // 2, IF_CAP + 1)
    spot = jax.random.randint(key_spot, (), 0, pairs)
    counts = counts.at[spot].set(IF_CAP)
    slots = jnp.arange(IF_CAP, dtype=jnp.int32)[None, :]
    filled = slots < counts[:, None]

    def first_bodies(one_key):
        return jax.random.permutation(one_key, B_SUB)[:IF_CAP].astype(jnp.int32)
    nexts = jax.vmap(first_bodies)(jax.random.split(key_next, SUBDOMAINS))
    prevs = jax.vmap(first_bodies)(jax.random.split(key_prev, SUBDOMAINS))
    empty_row = jnp.full((1, IF_CAP), B_SUB, jnp.int32)
    next_rows = jnp.where(filled, nexts[:-1], B_SUB).astype(jnp.int32)
    prev_rows = jnp.where(filled, prevs[1:], B_SUB).astype(jnp.int32)
    return (jnp.concatenate([next_rows, empty_row], axis=0), jnp.concatenate([empty_row, prev_rows], axis=0))


def draw_next_list(key, part):
    return interface_lists(key)[0]


def draw_prev_list(key, part):
    return interface_lists(key)[1]


def draw_contact_pair(key, part):
    key = jax.random.fold_in(key, 11)
    key_first, key_step = jax.random.split(key)
    first = jax.random.randint(key_first, (CONTACTS,), 0, B_SUB)
    step = jax.random.randint(key_step, (CONTACTS,), 1, B_SUB)
    second = (first + step) % B_SUB
    return jnp.stack([first, second]).astype(jnp.int32)


def draw_inverse_delassus(key, part):
    key = jax.random.fold_in(key, 23)
    key_diag, key_off = jax.random.split(key)
    diagonal = jnp.exp(jax.random.uniform(key_diag, (3, CONTACTS), jnp.float32, jnp.log(0.1), jnp.log(0.3)))
    off = jax.random.uniform(key_off, (3, 3, CONTACTS), jnp.float32, -0.04, 0.04)
    eye = jnp.eye(3, dtype=jnp.float32)[:, :, None]
    return (off * (1.0 - eye) + eye * diagonal[None, :, :]).astype(jnp.float32)


def plant(values, rng, smallest, high):
    index_at = [jax.random.randint(jax.random.fold_in(rng, axis), (), 0, length) for axis, length in enumerate(values.shape)]
    main_axis = values.shape.index(max(values.shape))
    next_to = index_at[:main_axis] + [(index_at[main_axis] + 1) % values.shape[main_axis]] + index_at[main_axis + 1:]
    return values.at[tuple(index_at)].set(smallest).at[tuple(next_to)].set(high)


def levels(own_key, dims, cuts, low, top_value):
    def one(axis_at, parts):
        steps = jax.random.uniform(jax.random.fold_in(jax.random.fold_in(own_key, 6), axis_at), (parts,), jnp.float32, low / len(cuts), top_value / len(cuts))
        return jnp.repeat(jnp.exp(steps), dims[axis_at] // parts).reshape((-1,) + (1,) * (len(dims) - axis_at - 1))

    loudness = one(*cuts[0])
    for cut in cuts[1:]:
        loudness = loudness * one(*cut)
    return loudness


def bell_draw(stream_key, extent, width, most, cuts=(), kind=jnp.bfloat16):
    entries = jax.random.normal(stream_key, extent, jnp.float32) * width
    if len(cuts) > 0:
        entries = levels(stream_key, extent, cuts, -0.22, 0.18) * entries
    return jnp.clip(entries, min=-most, max=most).astype(kind)


def setup_inputs(seed: int = 0) -> dict:
    streams_of = jax.random.split(jax.random.key(seed), 14)
    free_velocity = bell_draw(streams_of[0], (6, BODIES), 1.0, 6.0, ((1, 32),), jnp.float32)
    inverse_mass = jnp.clip(jnp.exp(math.log(1.0) - 1.3862944 * jax.random.uniform(streams_of[1], (6, BODIES), jnp.float32) ** levels(streams_of[1], (6, BODIES), ((1, 32),), -0.2, 0.2)), 0.25, 1.0)
    contact_pair = draw_contact_pair(jax.random.fold_in(streams_of[13], 71), 0)
    jac_near = bell_draw(streams_of[3], (3, 6, CONTACTS), 6 ** -0.5, 2.5, ((2, 1024),), jnp.float32)
    jac_far = bell_draw(streams_of[4], (3, 6, CONTACTS), 6 ** -0.5, 2.5, ((2, 1024),), jnp.float32)
    inverse_delassus = draw_inverse_delassus(jax.random.fold_in(streams_of[13], 71), 0)
    friction = jnp.clip(jnp.exp(math.log(0.9) - 1.0986122 * jax.random.uniform(streams_of[6], (CONTACTS,), jnp.float32) ** levels(streams_of[6], (CONTACTS,), ((0, 1024),), -0.2, 0.2)), 0.3, 0.9)
    velocity_bias = bell_draw(streams_of[7], (3, CONTACTS), 1.0, 6.0, ((1, 1024),), jnp.float32)
    warm_reaction = bell_draw(streams_of[8], (3, CONTACTS), 0.3, 2.0, ((1, 1024),), jnp.float32)
    active_flag = plant((jax.random.randint(streams_of[9], (CONTACTS,), 0, 4) < 3).astype(jnp.int32), jax.random.fold_in(streams_of[9], 1), 0, 1)
    sticking_flag = plant((jax.random.randint(streams_of[10], (CONTACTS,), 0, 2) < 1).astype(jnp.int32), jax.random.fold_in(streams_of[10], 1), 0, 1)
    next_list = draw_next_list(jax.random.fold_in(streams_of[13], 71), 0)
    prev_list = draw_prev_list(jax.random.fold_in(streams_of[13], 71), 0)
    return dict(free_velocity=free_velocity, inverse_mass=inverse_mass, contact_pair=contact_pair, jac_near=jac_near, jac_far=jac_far, inverse_delassus=inverse_delassus, friction=friction, velocity_bias=velocity_bias, warm_reaction=warm_reaction, active_flag=active_flag, sticking_flag=sticking_flag, next_list=next_list, prev_list=prev_list)


def reference(free_velocity, inverse_mass, contact_pair, jac_near, jac_far, inverse_delassus, friction, velocity_bias, warm_reaction, active_flag, sticking_flag, next_list, prev_list):
    block = C_DEV * N_CON
    owner = (jnp.arange(CONTACTS, dtype=jnp.int32) // block) * B_SUB
    near = contact_pair[0] + owner
    far = contact_pair[1] + owner
    both_ends = jnp.concatenate([near, far]).astype(jnp.int32)
    offset = (jnp.arange(SUBDOMAINS, dtype=jnp.int32) * B_SUB)[:, None]
    next_global = jnp.where(next_list < B_SUB, next_list + offset, BODIES).reshape(-1)
    prev_global = jnp.where(prev_list < B_SUB, prev_list + offset, BODIES).reshape(-1)
    slots_all = jnp.concatenate([next_global, prev_global]).astype(jnp.int32)
    shared = jnp.ones((BODIES,), jnp.float32).at[slots_all].add(1.0, mode="drop")
    bound_scale = friction * (1.0 + 0.5 * sticking_flag.astype(jnp.float32))
    live = active_flag.astype(jnp.float32)

    def velocity_of(reaction):
        term_near = jnp.sum(jac_near * reaction[:, None, :], axis=0)
        term_far = jnp.sum(jac_far * reaction[:, None, :], axis=0)
        terms = jnp.concatenate([term_near, term_far], axis=1)
        impulse = jnp.zeros((6, BODIES), jnp.float32).at[:, both_ends].add(terms)
        own = free_velocity + inverse_mass * impulse
        outgoing = jnp.take(own, slots_all, axis=1, mode="fill", fill_value=0.0)
        count = SUBDOMAINS * IF_CAP
        to_next = outgoing[:, :count].reshape(6, SUBDOMAINS, IF_CAP)
        to_prev = outgoing[:, count:].reshape(6, SUBDOMAINS, IF_CAP)
        empty = jnp.zeros((6, 1, IF_CAP), jnp.float32)
        from_next = jnp.concatenate([to_prev[:, 1:], empty], axis=1).reshape(6, -1)
        from_prev = jnp.concatenate([empty, to_next[:, :-1]], axis=1).reshape(6, -1)
        incoming = jnp.concatenate([from_next, from_prev], axis=1)
        total = own.at[:, slots_all].add(incoming, mode="drop")
        return total / shared

    def update(velocity, reaction):
        ends_vel = jnp.take(velocity, both_ends, axis=1)
        near_vel = ends_vel[:, :CONTACTS]
        far_vel = ends_vel[:, CONTACTS:]
        relative = jnp.sum(jac_near * near_vel[None], axis=1) + jnp.sum(jac_far * far_vel[None], axis=1) + velocity_bias
        trial = reaction - jnp.sum(inverse_delassus * relative[None, :, :], axis=1)
        normal = jnp.maximum(trial[0], 0.0)
        limit = bound_scale * normal
        tangent = jnp.clip(trial[1:], -limit, limit)
        return jnp.concatenate([normal[None], tangent], axis=0) * live

    reaction = warm_reaction
    for step in range(PASSES):
        velocity = velocity_of(reaction)
        reaction = update(velocity, reaction)
    velocity = velocity_of(reaction)
    return velocity, reaction
```

```python
import jax
import jax.numpy as jnp
from jax import lax
from jax.experimental import pallas as pl
from jax.experimental.pallas import tpu as pltpu
from jax.sharding import PartitionSpec as P

PASSES = 3
EVALS = PASSES + 1
N_CON = 32
BODIES = 2048
CONTACTS = 512
ENDS = 2 * CONTACTS
SLOTS = 256
HIGH = 8
LOW = 256
TILES = 16
MESH = pl.DeviceIdType.MESH
F32 = jnp.float32
BF16 = jnp.bfloat16
OFFSETS = sorted(range(1, N_CON), key=lambda k: -min(k, N_CON - k))


def body_owner(tile):
    return (tile // 4) * 8 + 2 + tile % 4


def two_parts(values):
    rest = values - values.astype(BF16).astype(F32)
    return jnp.concatenate([values, rest], axis=0).astype(BF16)


def dot(a, b):
    return lax.dot_general(a, b, (((1,), (0,)), ((), ())), preferred_element_type=F32)


def join(parts):
    return parts[0:8] + parts[8:16]


def kernel(
    fv, im, pair, jn, jf, invd, fric, bias, warm, act, stick, nxt, prv,
    vel_out, react_out,
    jac, mask, oh_low, oh_next, oh_prev, low_oh, next_oh, prev_oh,
    slot_oh, slot_mask, inv_ends, inv_body, own_fv, own_im, react,
    part, rs, acc, ag,
    rs_send, rs_recv, ag_send, body_recv, slot_recv,
):
    sub = lax.axis_index("sub")
    con = lax.axis_index("con")
    subs = lax.axis_size("sub")
    after = lax.rem(sub + 1, subs)
    before = lax.rem(sub + subs - 1, subs)
    x8 = (con // 8) * 8
    z = lax.rem(con // 2, 4)
    core = lax.rem(con, 2)
    my_tile = (con // 8) * 4 + (z - 1) * 2 + core
    owns_body = jnp.logical_and(z >= 1, z <= 2)

    ag[...] = jnp.zeros_like(ag)

    barrier = pltpu.get_barrier_semaphore()
    for k in OFFSETS:
        pl.semaphore_signal(barrier, inc=1, device_id=(sub, lax.rem(con + k, N_CON)), device_id_type=MESH)
    for c in range(2):
        pl.semaphore_signal(barrier, inc=1, device_id=(before, x8 + 6 + c), device_id_type=MESH)
        pl.semaphore_signal(barrier, inc=1, device_id=(after, x8 + c), device_id_type=MESH)

    ends_row = jnp.concatenate([pair[0:1, :], pair[1:2, :]], axis=1)
    ends_f = jnp.broadcast_to(ends_row.astype(F32), (8, ENDS))
    ends_col = ends_f.T[:, 0:1].astype(jnp.int32)
    high_row = ends_row // LOW
    low_row = ends_row - high_row * LOW
    low_col = lax.rem(ends_col, LOW)
    oh_low[...] = (lax.broadcasted_iota(jnp.int32, (ENDS, LOW), 1) == low_col).astype(F32).astype(BF16)
    oh_next[...] = (nxt[...] == ends_col).astype(F32).astype(BF16)
    oh_prev[...] = (prv[...] == ends_col).astype(F32).astype(BF16)
    for h in range(HIGH):
        mask[h * 16:(h + 1) * 16, :] = jnp.broadcast_to((high_row == h).astype(F32), (16, ENDS)).astype(BF16)
    jac[...] = jnp.zeros_like(jac)
    jac[:, 0:6, 0:CONTACTS] = jn[...]
    jac[:, 0:6, CONTACTS:ENDS] = jf[...]
    react[...] = warm[...]

    def make_sums(e):
        reaction = react[...]
        both = jnp.concatenate([reaction, reaction], axis=1)
        terms = jac[0] * both[0:1] + jac[1] * both[1:2] + jac[2] * both[2:3]
        parts = two_parts(terms)
        to_next = join(dot(parts, oh_next[...]))
        to_prev = join(dot(parts, oh_prev[...]))
        for x in range(4):
            for c in range(2):
                part[e, x * 8 + 6 + c] = to_next[:, c * 128:(c + 1) * 128]
                part[e, x * 8 + c] = to_prev[:, c * 128:(c + 1) * 128]
        spread = jnp.concatenate([parts] * HIGH, axis=0) * mask[...]
        sums = dot(spread, oh_low[...])
        for t in range(TILES):
            rows = join(sums[(t // 2) * 16:(t // 2 + 1) * 16])
            part[e, body_owner(t)] = rows[:, (t % 2) * 128:(t % 2 + 1) * 128]

    def sum_copy(e, k):
        to = lax.rem(con + k, N_CON)
        return pltpu.make_async_remote_copy(
            src_ref=part.at[e, to, pl.ds(0, 6)], dst_ref=rs.at[e, k, pl.ds(0, 6)],
            send_sem=rs_send.at[e], recv_sem=rs_recv.at[e], device_id=(sub, to), device_id_type=MESH)

    def body_copy(e, k):
        return pltpu.make_async_remote_copy(
            src_ref=acc.at[e, pl.ds(0, 6)], dst_ref=ag.at[e, my_tile, pl.ds(0, 6)],
            send_sem=ag_send.at[e], recv_sem=body_recv.at[e],
            device_id=(sub, lax.rem(con + k, N_CON)), device_id_type=MESH)

    def slot_copy(e, to_sub, base, q):
        return pltpu.make_async_remote_copy(
            src_ref=acc.at[e, pl.ds(0, 6)], dst_ref=ag.at[e, base + core, pl.ds(0, 6)],
            send_sem=ag_send.at[e], recv_sem=slot_recv.at[e],
            device_id=(to_sub, x8 + q), device_id_type=MESH)

    def all_of(ref, send, recv):
        return pltpu.make_async_remote_copy(
            src_ref=ref, dst_ref=ref, send_sem=send, recv_sem=recv,
            device_id=(sub, lax.rem(con + 1, N_CON)), device_id_type=MESH)

    def send_sums(e):
        for k in OFFSETS:
            sum_copy(e, k).start()

    def exchange(e):
        all_of(rs.at[e, pl.ds(1, N_CON - 1), pl.ds(0, 6)], rs_send.at[e], rs_recv.at[e]).wait_recv()
        impulse = jnp.sum(rs[e, 1:N_CON], axis=0) + part[e, con]
        mine = own_fv[con] + own_im[con] * impulse
        acc[e] = mine

        @pl.when(z == 3)
        def _():
            for q in range(8):
                slot_copy(e, after, 18, q).start()

        @pl.when(z == 0)
        def _():
            for q in range(8):
                slot_copy(e, before, 16, q).start()

        @pl.when(owns_body)
        def _():
            for k in OFFSETS:
                body_copy(e, k).start()
            ag[e, my_tile, 0:6] = mine[0:6]
            all_of(ag.at[e, pl.ds(0, TILES - 1), pl.ds(0, 6)], ag_send.at[e], body_recv.at[e]).wait_recv()

        @pl.when(jnp.logical_not(owns_body))
        def _():
            all_of(ag.at[e, pl.ds(0, TILES), pl.ds(0, 6)], ag_send.at[e], body_recv.at[e]).wait_recv()

    def wait_slots(e):
        all_of(ag.at[e, pl.ds(TILES, 4), pl.ds(0, 6)], ag_send.at[e], slot_recv.at[e]).wait_recv()

    def wide(e, tile):
        return jnp.concatenate([ag[e, tile], ag[e, tile + 1]], axis=1)

    def update(e):
        table = jnp.concatenate([two_parts(wide(e, 2 * h)) for h in range(HIGH)], axis=0)
        got = dot(table, low_oh[...])
        at_ends = jnp.zeros((8, ENDS), F32)
        for h in range(HIGH):
            at_ends = jnp.where(high_row == h, join(got[h * 16:(h + 1) * 16]), at_ends)
        wait_slots(e)
        at_ends = at_ends + join(dot(two_parts(wide(e, 16)), next_oh[...]))
        at_ends = at_ends + join(dot(two_parts(wide(e, 18)), prev_oh[...]))
        at_ends = at_ends * inv_ends[...]
        reaction = react[...]
        relative = []
        for i in range(3):
            moved = jnp.sum(jac[i] * at_ends, axis=0, keepdims=True)
            relative.append(moved[:, 0:CONTACTS] + moved[:, CONTACTS:ENDS] + bias[i:i + 1, :])
        trial = []
        for i in range(3):
            step = invd[i, 0:1, :] * relative[0] + invd[i, 1:2, :] * relative[1] + invd[i, 2:3, :] * relative[2]
            trial.append(reaction[i:i + 1, :] - step)
        live = act[...].astype(F32)
        normal = jnp.maximum(trial[0], 0.0)
        limit = fric[...] * (1.0 + 0.5 * stick[...].astype(F32)) * normal
        react[0:1, :] = normal * live
        react[1:2, :] = jnp.minimum(jnp.maximum(trial[1], -limit), limit) * live
        react[2:3, :] = jnp.minimum(jnp.maximum(trial[2], -limit), limit) * live

    make_sums(0)
    pl.semaphore_wait(barrier, N_CON - 1 + jnp.where(owns_body, 0, 8))
    send_sums(0)

    rows_low = lax.broadcasted_iota(jnp.int32, (LOW, ENDS), 0)
    low_oh[...] = (rows_low == low_row).astype(F32).astype(BF16)
    lists_row = jnp.concatenate([nxt[...], prv[...]], axis=1)
    lists_f = jnp.broadcast_to(lists_row.astype(F32), (8, 2 * SLOTS))
    lists_col = lists_f.T[:, 0:1].astype(jnp.int32)
    next_oh[...] = (lists_col[0:SLOTS] == ends_row).astype(F32).astype(BF16)
    prev_oh[...] = (lists_col[SLOTS:2 * SLOTS] == ends_row).astype(F32).astype(BF16)
    ones = jnp.ones((16, SLOTS), BF16)
    inv_ends[...] = 1.0 / (1.0 + dot(ones, next_oh[...])[0:8] + dot(ones, prev_oh[...])[0:8])
    slot_high = lists_row // LOW
    slot_low = lists_row - slot_high * LOW
    slot_oh[...] = (lax.broadcasted_iota(jnp.int32, (2 * SLOTS, LOW), 1) == lax.rem(lists_col, LOW)).astype(F32).astype(BF16)
    for h in range(HIGH):
        slot_mask[h * 16:(h + 1) * 16, :] = jnp.broadcast_to((slot_high == h).astype(F32), (16, 2 * SLOTS)).astype(BF16)
    counts = dot(slot_mask[...], slot_oh[...])
    for h in range(HIGH):
        inv_body[h] = 1.0 / (1.0 + counts[h * 16:h * 16 + 8])
    low_slot = (lax.broadcasted_iota(jnp.int32, (LOW, 2 * SLOTS), 0) == slot_low).astype(F32).astype(BF16)
    for source, own in ((fv, own_fv), (im, own_im)):
        at_slots = jnp.zeros((8, 2 * SLOTS), F32)
        for h in range(HIGH):
            chunk = jnp.concatenate([source[:, h * LOW:(h + 1) * LOW], jnp.zeros((2, LOW), F32)], axis=0)
            own[body_owner(2 * h)] = chunk[:, 0:128]
            own[body_owner(2 * h + 1)] = chunk[:, 128:256]
            at_slots = jnp.where(slot_high == h, join(dot(two_parts(chunk), low_slot)), at_slots)
        for x in range(4):
            for c in range(2):
                own[x * 8 + 6 + c] = at_slots[:, c * 128:(c + 1) * 128]
                own[x * 8 + c] = at_slots[:, SLOTS + c * 128:SLOTS + (c + 1) * 128]

    def one_pass(e, _):
        exchange(e)
        update(e)
        make_sums(e + 1)
        send_sums(e + 1)
        return 0

    lax.fori_loop(0, PASSES, one_pass, 0)
    react_out[...] = react[...]
    exchange(PASSES)
    wait_slots(PASSES)
    incoming = two_parts(jnp.concatenate([wide(PASSES, 16), wide(PASSES, 18)], axis=1))
    added = dot(jnp.concatenate([incoming] * HIGH, axis=0) * slot_mask[...], slot_oh[...])
    for h in range(HIGH):
        total = (wide(PASSES, 2 * h) + join(added[h * 16:(h + 1) * 16])) * inv_body[h]
        vel_out[:, h * LOW:(h + 1) * LOW] = total[0:6]

    def drain(e, _):
        all_of(rs.at[e, pl.ds(1, N_CON - 1), pl.ds(0, 6)], rs_send.at[e], rs_recv.at[e]).wait_send()

        @pl.when(owns_body)
        def _():
            all_of(rs.at[e, pl.ds(1, N_CON - 1), pl.ds(0, 6)], ag_send.at[e], rs_recv.at[e]).wait_send()

        @pl.when(jnp.logical_not(owns_body))
        def _():
            all_of(rs.at[e, pl.ds(1, 8), pl.ds(0, 6)], ag_send.at[e], rs_recv.at[e]).wait_send()

        return 0

    lax.fori_loop(0, EVALS, drain, 0)


def body(
    free_velocity, inverse_mass, contact_pair, jac_near, jac_far, inverse_delassus, friction,
    velocity_bias, warm_reaction, active_flag, sticking_flag, next_list, prev_list,
):
    vmem = pl.BlockSpec(memory_space=pltpu.VMEM)
    tile = (8, 128)
    return pl.pallas_call(
        kernel,
        out_shape=(
            jax.ShapeDtypeStruct((6, BODIES), F32),
            jax.ShapeDtypeStruct((3, CONTACTS), F32),
        ),
        in_specs=[vmem] * 13,
        out_specs=(vmem, vmem),
        scratch_shapes=[
            pltpu.VMEM((3, 8, ENDS), F32),
            pltpu.VMEM((HIGH * 16, ENDS), BF16),
            pltpu.VMEM((ENDS, LOW), BF16),
            pltpu.VMEM((ENDS, SLOTS), BF16),
            pltpu.VMEM((ENDS, SLOTS), BF16),
            pltpu.VMEM((LOW, ENDS), BF16),
            pltpu.VMEM((SLOTS, ENDS), BF16),
            pltpu.VMEM((SLOTS, ENDS), BF16),
            pltpu.VMEM((2 * SLOTS, LOW), BF16),
            pltpu.VMEM((HIGH * 16, 2 * SLOTS), BF16),
            pltpu.VMEM((8, ENDS), F32),
            pltpu.VMEM((HIGH, 8, LOW), F32),
            pltpu.VMEM((N_CON,) + tile, F32),
            pltpu.VMEM((N_CON,) + tile, F32),
            pltpu.VMEM((3, CONTACTS), F32),
            pltpu.VMEM((EVALS, N_CON) + tile, F32),
            pltpu.VMEM((EVALS, N_CON) + tile, F32),
            pltpu.VMEM((EVALS,) + tile, F32),
            pltpu.VMEM((EVALS, TILES + 4) + tile, F32),
            pltpu.SemaphoreType.DMA((EVALS,)),
            pltpu.SemaphoreType.DMA((EVALS,)),
            pltpu.SemaphoreType.DMA((EVALS,)),
            pltpu.SemaphoreType.DMA((EVALS,)),
            pltpu.SemaphoreType.DMA((EVALS,)),
        ],
        compiler_params=pltpu.CompilerParams(
            collective_id=0, has_side_effects=True, vmem_limit_bytes=32 * 1024 * 1024),
    )(
        free_velocity, inverse_mass, contact_pair, jac_near, jac_far, inverse_delassus,
        friction[None, :], velocity_bias, warm_reaction, active_flag[None, :], sticking_flag[None, :],
        next_list, prev_list,
    )


def solution(mesh):
    in_specs = (
        P(None, "sub"),
        P(None, "sub"),
        P(None, ("sub", "con")),
        P(None, None, ("sub", "con")),
        P(None, None, ("sub", "con")),
        P(None, None, ("sub", "con")),
        P(("sub", "con")),
        P(None, ("sub", "con")),
        P(None, ("sub", "con")),
        P(("sub", "con")),
        P(("sub", "con")),
        P("sub", None),
        P("sub", None),
    )
    out_specs = (P(None, "sub"), P(None, ("sub", "con")))
    return jax.shard_map(body, mesh=mesh, in_specs=in_specs, out_specs=out_specs, check_vma=False)
```
